32 devices in a mesh: dp: 2 (over y), panel: 16 (over z, x, core).
Axes of the slice: x: 2, y: 2, z: 4, core: 2. Of those that a mesh axis runs over, the one named last changes fastest.
Arguments:
- tokens: bfloat16 [512, 6144], P('dp'), may hold values from -8 to 8
- out_grads: bfloat16 [512, 6144], P('dp'), may hold values from -8 to 8
- basis_in: bfloat16 [6144, 6144], P(None, 'panel'), may hold values from -0.078125 to 0.078125
- basis_out: bfloat16 [6144, 6144], P(None, 'panel'), may hold values from -0.078125 to 0.078125
Outputs:
- update: bfloat16 [6144, 6144], P('panel', 'dp')
The draws below stay inside these ranges and needn't reach their ends.
All inputs are finite; a program needn't handle non-finite values.
Results may differ from the reference program's by a relative error of at most 0.012.
Values may be sent and summed in bfloat16 or wider, within the bound.
No kernel may reach another device: no remote copies, remote signals or barrier semaphores. Data moves between devices by JAX's collectives and lax.ppermute only.
A program may use at most 128 MiB of HBM per device.

```python
import math
import jax
import jax.numpy as jnp
from jax import lax

D = 6144
TOKENS = 512
N_DP = 2


def shared_factors(key):
    common_key = jax.random.fold_in(key, 5)
    key_scale, key_latent = jax.random.split(common_key, 2)
    scale = jnp.exp(jax.random.uniform(key_scale, (TOKENS, 1), jnp.float32, math.log(0.25), math.log(4.0)))
    latent = jax.random.normal(key_latent, (TOKENS, 8), jnp.float32)
    return (scale, latent)


def draw_mixture(key, salt_value):
    scale, latent = shared_factors(key)
    mixed_key = jax.random.fold_in(key, salt_value)
    key_center, key_spread, key_mixing = jax.random.split(mixed_key, 3)
    center = jax.random.normal(key_center, (1, D), jnp.float32)
    mixing = jax.random.normal(key_mixing, (8, D), jnp.float32) / math.sqrt(8.0)
    spread_part = jax.random.normal(key_spread, (TOKENS, D), jnp.float32)
    shared_part = jnp.dot(latent, mixing, precision=jax.lax.Precision.HIGHEST)
    values = center + scale * (spread_part + shared_part)
    return jnp.clip(values, -8.0, 8.0).astype(jnp.bfloat16)


def draw_tokens(key, part):
    return draw_mixture(key, 11)


def draw_out_grads(key, part):
    return draw_mixture(key, 23)


def steps_of(stream_key, dims, cuts, smallest, largest):
    def one(dim, parts):
        draws = jax.random.uniform(jax.random.fold_in(jax.random.fold_in(stream_key, 6), dim), (parts,), jnp.float32, smallest / len(cuts), largest / len(cuts))
        return jnp.repeat(jnp.exp(draws), dims[dim] // parts).reshape((-1,) + (1,) * (len(dims) - dim - 1))

    factor_of = one(*cuts[0])
    for cut in cuts[1:]:
        factor_of = factor_of * one(*cut)
    return factor_of


def gaussian(own_key, shape, width, most, shards=(), kind=jnp.bfloat16):
    result = width * jax.random.normal(own_key, shape, jnp.float32)
    if shards:
        result = result * steps_of(own_key, shape, shards, -0.22, 0.18)
    return jnp.clip(result, -most, most).astype(kind)


def setup_inputs(seed: int = 0) -> dict:
    seeds = jax.random.split(jax.random.key(seed), 5)
    return {
        "tokens": draw_tokens(jax.random.fold_in(seeds[4], 71), 0),
        "out_grads": draw_out_grads(jax.random.fold_in(seeds[4], 71), 0),
        "basis_in": gaussian(seeds[2], (D, D), D ** -0.5, 0.078125, ((1, 16),)),
        "basis_out": gaussian(seeds[3], (D, D), D ** -0.5, 0.078125, ((1, 16),)),
    }


damping = 0.1


def reference(tokens, out_grads, basis_in, basis_out):
    proj_in = jnp.dot(tokens, basis_in, preferred_element_type=jnp.float32).astype(jnp.bfloat16)
    proj_out = jnp.dot(out_grads, basis_out, preferred_element_type=jnp.float32).astype(jnp.bfloat16)
    sq_in = (proj_in.astype(jnp.float32) ** 2).astype(jnp.bfloat16)
    sq_out = (proj_out.astype(jnp.float32) ** 2).astype(jnp.bfloat16)
    group_rows = TOKENS // N_DP
    contract = (((0,), (0,)), ((), ()))

    def group_sum(carry, index):
        first = (index * group_rows).astype(jnp.int32)
        seg_in = lax.dynamic_slice_in_dim(proj_in, first, group_rows, 0)
        seg_out = lax.dynamic_slice_in_dim(proj_out, first, group_rows, 0)
        sqr_in = lax.dynamic_slice_in_dim(sq_in, first, group_rows, 0)
        sqr_out = lax.dynamic_slice_in_dim(sq_out, first, group_rows, 0)
        product = lax.dot_general(seg_in, seg_out, contract, preferred_element_type=jnp.float32) / TOKENS
        square = lax.dot_general(sqr_in, sqr_out, contract, preferred_element_type=jnp.float32) / TOKENS
        product = lax.optimization_barrier(product.astype(jnp.bfloat16)).astype(jnp.float32)
        square = lax.optimization_barrier(square.astype(jnp.bfloat16)).astype(jnp.float32)
        return (carry[0] + product, carry[1] + square), None

    initial = (jnp.zeros((D, D), jnp.float32), jnp.zeros((D, D), jnp.float32))
    (summed, corrections), _ = lax.scan(group_sum, initial, jnp.arange(N_DP, dtype=jnp.int32))
    ratio = (summed / (corrections + damping)).astype(jnp.bfloat16)
    rotated = jnp.dot(ratio, basis_out.T, preferred_element_type=jnp.float32).astype(jnp.bfloat16)
    return jnp.dot(basis_in, rotated, preferred_element_type=jnp.float32).astype(jnp.bfloat16)
```

```python
import jax
import jax.numpy as jnp
from jax import lax
from jax.sharding import PartitionSpec as P

damping = 0.1
pair = 2
chunks = 4
f32 = jnp.float32
bf16 = jnp.bfloat16


class Grid:
    def __init__(self):
        self.panel = lax.axis_size("panel")
        self.dp = lax.axis_size("dp")
        self.sizes = {"z": self.panel // (pair * pair), "x": pair, "c": pair}
        self.steps = {"z": pair * pair, "x": pair, "c": 1}
        p = lax.axis_index("panel")
        self.at = {k: (p // self.steps[k]) % self.sizes[k] for k in self.sizes}
        self.at["y"] = lax.axis_index("dp")
        self.sizes["y"] = self.dp

    def pairs(self, axis, shift, keep=None):
        size = self.sizes[axis]
        if axis == "y":
            return [((i + shift) % size, i) for i in range(size)]
        step = self.steps[axis]
        out = []
        for q in range(self.panel):
            i = (q // step) % size
            j = (i + shift) % size
            if keep is None or keep(j, i):
                out.append((q + (j - i) * step, q))
        return out

    def fetch(self, value, axis, shift, keep=None):
        name = "dp" if axis == "y" else "panel"
        return lax.ppermute(value, name, self.pairs(axis, shift, keep))

    def gather(self, value, axis):
        return [value] + [self.fetch(value, axis, s) for s in range(1, self.sizes[axis])]

    def gather_line(self, value):
        n = self.sizes["z"]
        if n < 4:
            return self.gather(value, "z")
        z = self.at["z"]
        out = {0: value}
        for s in list(range(2, n - 1)) + [1, n - 1]:
            out[s] = self.fetch(value, "z", s, lambda j, i: abs(j - i) < n - 1)
        relay = out[2] if n == 4 else jnp.where(z == 1, out[n - 2], out[2])
        ends = lambda j, i: (j, i) == (1, 0)
        low = set(self.pairs("z", 1, ends))
        high = set(self.pairs("z", n - 1, lambda j, i: (j, i) == (n - 2, n - 1)))
        far = lax.ppermute(relay, "panel", sorted(low | high))
        out[1] = jnp.where(z == n - 1, far, out[1])
        out[n - 1] = jnp.where(z == 0, far, out[n - 1])
        return [out[s] for s in range(n)]


def dot(a, b, contract):
    return lax.dot_general(a, b, (contract, ((), ())), preferred_element_type=f32)


def shards(tokens, out_grads, basis_in, basis_out):
    grid = Grid()
    at, sizes = grid.at, grid.sizes
    nz, ny = sizes["z"], sizes["y"]
    width, cols = basis_in.shape
    tok_total = tokens.shape[0] * ny

    quarter = width // nz
    eighth = quarter // ny
    in_blocks = []
    for s in range(nz):
        to = (at["z"] + nz - s) % nz
        block = lax.dynamic_slice_in_dim(basis_in, to * quarter + at["y"] * eighth, eighth, 0)
        in_blocks.append(block if s == 0 else grid.fetch(block, "z", s))
    in_rows = jnp.concatenate(in_blocks, axis=1)
    in_rows = jnp.concatenate(grid.gather(in_rows, "x"), axis=1)

    proj_in = jnp.dot(tokens, basis_in, preferred_element_type=f32).astype(bf16)
    proj_out = jnp.dot(out_grads, basis_out, preferred_element_type=f32).astype(bf16)
    both = jnp.concatenate([proj_in, proj_out], axis=0)
    both = jnp.concatenate(grid.gather_line(both), axis=1)
    both = jnp.stack(grid.gather(both, "y"))
    rows = tokens.shape[0]
    left = both[:, :rows].reshape(tok_total, -1)
    right = both[:, rows:].reshape(tok_total, -1)
    left = jnp.concatenate(grid.gather(left, "x"), axis=1)
    right = jnp.concatenate(grid.gather(right, "c"), axis=1)

    square = lambda v: (v.astype(f32) ** 2).astype(bf16)
    summed = dot(left, right, ((0,), (0,))) / tok_total
    corrections = dot(square(left), square(right), ((0,), (0,))) / tok_total
    ratio = (summed / (corrections + damping)).astype(bf16)

    part = dot(in_rows, ratio, ((1,), (0,)))
    half = part.shape[1] // sizes["c"]
    mixed = part[:, :half]
    for s in range(1, sizes["c"]):
        mixed = mixed + grid.fetch(part[:, s * half : (s + 1) * half].astype(bf16), "c", s).astype(f32)
    mixed = mixed.astype(bf16)
    full = jnp.zeros((quarter, half), bf16)
    for s, block in enumerate(grid.gather(mixed, "y")):
        full = lax.dynamic_update_slice_in_dim(full, block, ((at["y"] + s) % ny) * eighth, 0)

    own = quarter // (pair * pair)
    ordered = [
        lax.dynamic_slice_in_dim(
            full, (((at["x"] + i) % pair) * pair + (at["c"] + j) % pair) * own, own, 0
        )
        for j in range(pair)
        for i in range(pair)
    ]
    near = jnp.concatenate(ordered[:pair], axis=0)
    away = jnp.concatenate(ordered[pair:], axis=0)

    out_rows = width // ny
    step = out_rows // chunks
    done = []
    for k in range(chunks):
        block = lax.dynamic_slice_in_dim(basis_out, at["y"] * out_rows + k * step, step, 0)
        block = jnp.concatenate(grid.gather_line(block), axis=1)
        given = dot(away, block, ((1,), (1,))).astype(bf16)
        kept = dot(near, block, ((1,), (1,)))
        kept = kept + grid.fetch(given, "c", 1).astype(f32)
        other = grid.fetch(kept[own:].astype(bf16), "x", 1)
        done.append((kept[:own] + other.astype(f32)).astype(bf16))
    return jnp.concatenate(done, axis=1)


def solution(mesh):
    return jax.shard_map(
        shards,
        mesh=mesh,
        in_specs=(P("dp", None), P("dp", None), P(None, "panel"), P(None, "panel")),
        out_specs=P("panel", "dp"),
        check_vma=False,
    )
```

```python
import jax
import jax.numpy as jnp
from jax import lax
from jax.experimental import pallas as pl
from jax.experimental.pallas import tpu as pltpu
from jax.sharding import PartitionSpec as P

damping = 0.1
pair = 2
shares = (5, 1)
f32 = jnp.float32
bf16 = jnp.bfloat16
params = pltpu.CompilerParams(vmem_limit_bytes=48 * 2**20)


def pairs(size, shift):
    return [((i + shift) % size, i) for i in range(size)]


def fetch(value, axis, shift=1):
    return lax.ppermute(value, axis, pairs(lax.axis_size(axis), shift))


def gather(value, axis):
    return [value] + [fetch(value, axis, s) for s in range(1, lax.axis_size(axis))]


def dot(a, b, contract):
    return lax.dot_general(a, b, (contract, ((), ())), preferred_element_type=f32)


def after(value, *others):
    return pl.pallas_call(
        lambda *refs: None,
        out_shape=jax.ShapeDtypeStruct(value.shape, value.dtype),
        in_specs=[pl.BlockSpec(memory_space=pl.ANY)] * (1 + len(others)),
        out_specs=pl.BlockSpec(memory_space=pl.ANY),
        input_output_aliases={0: 0},
    )(value, *others)


def square(v):
    return (v.astype(f32) ** 2).astype(bf16)


def tile(size, most):
    fits = [t for t in range(128, most + 1, 128) if size % t == 0]
    return max(fits) if fits else size


def pack(groups, others, rows):
    count, wide = len(groups), len(groups[0])
    cols = groups[0][0].shape[1]

    def body(*refs):
        left_ref, other_ref, right_ref = refs[-3:]
        for s in range(count):
            for g in range(wide):
                ref = refs[s * wide + g]
                span = slice(g * rows, (g + 1) * rows)
                left_ref[s, :, span] = ref[:rows, :].T
                right_ref[span, s * cols : (s + 1) * cols] = ref[rows:, :]
                other_ref[s, :, span] = refs[(count + s) * wide + g][...].T

    left = jax.ShapeDtypeStruct((count, cols, wide * rows), bf16)
    return pl.pallas_call(
        body,
        out_shape=[left, left, jax.ShapeDtypeStruct((wide * rows, count * cols), bf16)],
        compiler_params=params,
    )(*[v for group in groups + others for v in group])


def mix(rows, left, rights, first, part, parts, kind, carry=None):
    count, cols, tok = left.shape
    n = rows[0].shape[0]
    span = rights[0].shape[1] // parts
    tj = tile(span, 768)
    runs = span // tj
    group = 2 if count % 2 == 0 and cols % 128 == 0 else 1

    def body(first_ref, *refs):
        row_refs, left_ref, refs = refs[:count], refs[count], refs[count + 1 :]
        right_refs, out_ref = refs[: len(rights)], refs[-1]
        j = pl.program_id(0)
        b = jnp.where(j // runs == first_ref[0], right_refs[0][...], right_refs[1][...])
        b2 = square(b)
        total = refs[len(rights)][...] if carry is not None else None
        for k in range(0, count, group):
            a = left_ref[k : k + group].reshape(group * cols, tok)
            summed = jnp.dot(a, b, preferred_element_type=f32)
            moment = jnp.dot(square(a), b2, preferred_element_type=f32)
            ratio = (summed / (moment + damping * tok)).astype(bf16)
            lead = [row_refs[k + i][...] for i in range(group)]
            lead = jnp.concatenate(lead, axis=1) if group > 1 else lead[0]
            step = jnp.dot(lead, ratio, preferred_element_type=f32)
            total = step if total is None else total + step
        out_ref[...] = total.astype(kind)

    specs = [pl.BlockSpec((n, cols), lambda j, f: (0, 0)) for _ in rows]
    specs += [pl.BlockSpec((count, cols, tok), lambda j, f: (0, 0, 0))]
    specs += [pl.BlockSpec((tok, tj), lambda j, f: (0, part * runs + j % runs)) for _ in rights]
    args = [*rows, left, *rights]
    if carry is not None:
        specs.append(pl.BlockSpec((n, tj), lambda j, f: (0, j)))
        args.append(carry)
    return pl.pallas_call(
        body,
        out_shape=jax.ShapeDtypeStruct((n, span * len(rights)), kind),
        grid_spec=pltpu.PrefetchScalarGridSpec(
            num_scalar_prefetch=1,
            grid=(runs * len(rights),),
            in_specs=specs,
            out_specs=pl.BlockSpec((n, tj), lambda j, f: (0, j)),
        ),
        compiler_params=params,
    )(jnp.full((1,), first, jnp.int32), *args)


def expand(halves, pick, blocks, order, kind, extra=None):
    _, n, deep = halves[0].shape
    count, wide, cols = blocks.shape
    steps = count // len(halves)
    scalars = jnp.concatenate([order, jnp.full((1,), pick, jnp.int32)])

    def body(scalar_ref, *refs):
        lefts, rights = refs[: len(halves)], refs[len(halves) : 2 * len(halves)]
        out_ref, total = refs[-2:]
        k = pl.program_id(0)
        if cols % 128 == 0:
            left = jnp.concatenate([r[0] for r in lefts], axis=1)
            right = jnp.concatenate([r[0] for r in rights], axis=1)
            step = dot(left, right, ((1,), (1,)))
        else:
            step = sum(dot(a[0, 0], b[0], ((1,), (1,))) for a, b in zip(lefts, rights))

        @pl.when(k == 0)
        def _():
            total[...] = step + refs[2 * len(halves)][...].astype(f32) if extra is not None else step

        @pl.when(k > 0)
        def _():
            total[...] += step

        @pl.when(k == steps - 1)
        def _():
            out_ref[...] = total[...].astype(kind)

    if cols % 128 == 0:
        specs = [pl.BlockSpec((1, n, cols), lambda k, s: (s[count], 0, k)) for _ in halves]
    else:
        halves = [h.reshape(h.shape[0], n, steps, cols).transpose(0, 2, 1, 3) for h in halves]
        specs = [pl.BlockSpec((1, 1, n, cols), lambda k, s: (s[count], k, 0, 0)) for _ in halves]
    for h in range(len(halves)):
        specs.append(pl.BlockSpec((1, wide, cols), lambda k, s, h=h: (s[h * steps + k], 0, 0)))
    args = [*halves, *[blocks] * len(halves)]
    if extra is not None:
        specs.append(pl.BlockSpec((n, wide), lambda k, s: (0, 0)))
        args.append(extra)
    return pl.pallas_call(
        body,
        out_shape=jax.ShapeDtypeStruct((n, wide), kind),
        grid_spec=pltpu.PrefetchScalarGridSpec(
            num_scalar_prefetch=1,
            grid=(steps,),
            in_specs=specs,
            out_specs=pl.BlockSpec((n, wide), lambda k, s: (0, 0)),
            scratch_shapes=[pltpu.VMEM((n, wide), f32)],
        ),
        compiler_params=params,
    )(scalars, *args)


def shards(tokens, out_grads, basis_in, basis_out):
    at = {k: lax.axis_index(k) for k in "yzxc"}
    nz, ny = lax.axis_size("z"), lax.axis_size("y")
    width, cols = basis_in.shape
    rows = tokens.shape[0]
    quarter = width // nz
    eighth = quarter // ny

    proj_in = jnp.dot(tokens, basis_in, preferred_element_type=f32).astype(bf16)
    proj_out = jnp.dot(out_grads, basis_out, preferred_element_type=f32).astype(bf16)
    both = jnp.concatenate([proj_in, proj_out], axis=0)
    order = [0] + sorted(range(1, nz), key=lambda s: -min(s, nz - s))
    groups, others, links = {}, {}, []
    for s in order:
        value = fetch(both, "z", s) if s else both
        links += [value] if s else []
        groups[s] = gather(value, "y")
        others[s] = gather(fetch(value[:rows], "x"), "y")
    every = range(nz)
    left, left_other, right = pack([groups[s] for s in every], [others[s] for s in every], rows)
    rights = [right, fetch(right, "c")]

    blocks = pair * pair
    share = quarter // (blocks * ny)
    in_view = basis_in.reshape(nz, blocks, ny, share, cols)
    in_own, in_other = {}, {}
    for s in order:
        to = (at["z"] + nz - s) % nz
        block = lax.dynamic_slice(in_view, (to, 0, at["y"], 0, 0), (1, blocks, 1, share, cols))
        block = block.reshape(eighth, cols)
        in_own[s] = fetch(after(block, *links, in_other[0]), "z", s) if s else block
        in_other[s] = fetch(in_own[s], "x")
    in_own = [in_own[s] for s in range(nz)]
    in_other = [in_other[s] for s in range(nz)]

    out_rows = width // ny
    cuts = [out_rows * sum(shares[:k]) // sum(shares) // 128 * 128 for k in range(len(shares))] + [out_rows]
    sizes = [b - a for a, b in zip(cuts, cuts[1:])]
    wides, gate = [], [*in_own[1:], left]
    for k in range(len(shares)):
        first = at["y"] * out_rows + cuts[k]
        raw = lax.dynamic_slice_in_dim(basis_out, first, sizes[k], 0)
        raw = after(raw, *gate) if gate else raw
        wides.append(lax.all_gather(raw, ("z", "c"), axis=0))

    parts = [mix(in_own, left, rights, at["c"], h, 2, f32) for h in range(2)]
    halves = []
    take = lambda v, axis, i: lax.dynamic_index_in_dim(v, i, axis, keepdims=False)
    for h in range(2):
        ready = after(left_other, mine) if h else left_other
        part = mix(in_other, ready, rights, at["c"], h, 2, bf16, parts[h])
        view = part.reshape(pair, pair, share, -1)
        away = fetch(take(view, 1, 1 - at["c"]), "c")
        mine = (take(view, 1, at["c"]).astype(f32) + away.astype(f32)).astype(bf16)
        got = gather(mine, "y")
        full = jnp.stack(
            [lax.select_n((ny + j - at["y"]) % ny, *got) if ny > 2 else
             jnp.where(at["y"] == j, got[0], got[-1]) for j in range(ny)], axis=1)
        halves.append(full.reshape(pair, ny * share, -1))
    place = [
        ((at["z"] + h * (nz // 2) + s) % nz) * pair + j
        for h in range(2) for j in range(pair) for s in range(nz // 2)
    ]
    place = jnp.stack(place).astype(jnp.int32)

    done = []
    for k in range(len(shares)):
        wide = after(wides[k], kept) if k else wides[k]
        given = fetch(expand(halves, 1 - at["x"], wide, place, bf16), "x")
        kept = expand(halves, at["x"], wide, place, f32)
        done.append((kept + given.astype(f32)).astype(bf16))
    return jnp.concatenate(done, axis=1)


def solution(mesh):
    sizes = (mesh.shape["dp"], mesh.shape["panel"] // (pair * pair), pair, pair)
    grid = jax.sharding.Mesh(mesh.devices.reshape(sizes), ("y", "z", "x", "c"))
    panels = ("z", "x", "c")
    return jax.shard_map(
        shards,
        mesh=grid,
        in_specs=(P("y", None), P("y", None), P(None, panels), P(None, panels)),
        out_specs=P(panels, "y"),
        check_vma=False,
    )
```

```python
import jax
import jax.numpy as jnp
from jax import lax
from jax.experimental import pallas as pl
from jax.experimental.pallas import tpu as pltpu
from jax.sharding import PartitionSpec as P

damping = 0.1
pair = 2
shares = (3, 1)
f32 = jnp.float32
bf16 = jnp.bfloat16
params = pltpu.CompilerParams(vmem_limit_bytes=48 * 2**20)


def pairs(size, shift):
    return [((i + shift) % size, i) for i in range(size)]


def fetch(value, axis, shift=1):
    return lax.ppermute(value, axis, pairs(lax.axis_size(axis), shift))


def gather(value, axis):
    return [value] + [fetch(value, axis, s) for s in range(1, lax.axis_size(axis))]


def dot(a, b, contract):
    return lax.dot_general(a, b, (contract, ((), ())), preferred_element_type=f32)


def after(value, *others):
    return pl.pallas_call(
        lambda *refs: None,
        out_shape=jax.ShapeDtypeStruct(value.shape, value.dtype),
        in_specs=[pl.BlockSpec(memory_space=pl.ANY)] * (1 + len(others)),
        out_specs=pl.BlockSpec(memory_space=pl.ANY),
        input_output_aliases={0: 0},
    )(value, *others)


def square(v):
    return (v.astype(f32) ** 2).astype(bf16)


def pack(groups, others, rows):
    count, wide = len(groups), len(groups[0])
    cols = groups[0][0].shape[1]

    def body(*refs):
        left_ref, other_ref, right_ref = refs[-3:]
        for s in range(count):
            for g in range(wide):
                ref = refs[s * wide + g]
                span = slice(g * rows, (g + 1) * rows)
                left_ref[s, :, span] = ref[:rows, :].T
                right_ref[span, s * cols : (s + 1) * cols] = ref[rows:, :]
                other_ref[s, :, span] = refs[(count + s) * wide + g][...].T

    left = jax.ShapeDtypeStruct((count, cols, wide * rows), bf16)
    return pl.pallas_call(
        body,
        out_shape=[left, left, jax.ShapeDtypeStruct((wide * rows, count * cols), bf16)],
        compiler_params=params,
    )(*[v for group in groups + others for v in group])


def mix(rows, left, rights, first, start, runs, kind, carry=None):
    count, cols, tok = left.shape
    n = rows[0].shape[0]
    tj = rights[0].shape[1] // 2
    group = 2 if count % 2 == 0 and cols % 128 == 0 else 1

    def body(first_ref, *refs):
        row_refs, left_ref, refs = refs[:count], refs[count], refs[count + 1 :]
        right_refs, out_ref = refs[: len(rights)], refs[-1]
        j = pl.program_id(0)
        b = jnp.where(j % 2 == first_ref[0], right_refs[0][...], right_refs[1][...])
        b2 = square(b)
        total = refs[len(rights)][...] if carry is not None else None
        for k in range(0, count, group):
            a = left_ref[k : k + group].reshape(group * cols, tok)
            summed = jnp.dot(a, b, preferred_element_type=f32)
            moment = jnp.dot(square(a), b2, preferred_element_type=f32)
            ratio = (summed / (moment + damping * tok)).astype(bf16)
            lead = [row_refs[k + i][...] for i in range(group)]
            lead = jnp.concatenate(lead, axis=1) if group > 1 else lead[0]
            step = jnp.dot(lead, ratio, preferred_element_type=f32)
            total = step if total is None else total + step
        out_ref[...] = total.astype(kind)

    specs = [pl.BlockSpec((n, cols), lambda j, f: (0, 0)) for _ in rows]
    specs += [pl.BlockSpec((count, cols, tok), lambda j, f: (0, 0, 0))]
    specs += [pl.BlockSpec((tok, tj), lambda j, f: (0, start + j // 2)) for _ in rights]
    args = [*rows, left, *rights]
    if carry is not None:
        specs.append(pl.BlockSpec((n, tj), lambda j, f: (0, 2 * start + j)))
        args.append(carry)
    return pl.pallas_call(
        body,
        out_shape=jax.ShapeDtypeStruct((n, 2 * runs * tj), kind),
        grid_spec=pltpu.PrefetchScalarGridSpec(
            num_scalar_prefetch=1,
            grid=(2 * runs,),
            in_specs=specs,
            out_specs=pl.BlockSpec((n, tj), lambda j, f: (0, j)),
        ),
        compiler_params=params,
    )(jnp.full((1,), first, jnp.int32), *args)


def expand(halves, pick, blocks, order, kind, extra=None):
    _, n, deep = halves[0].shape
    count, wide, cols = blocks.shape
    steps = count // len(halves)
    scalars = jnp.concatenate([order, jnp.full((1,), pick, jnp.int32)])

    def body(scalar_ref, *refs):
        lefts, rights = refs[: len(halves)], refs[len(halves) : 2 * len(halves)]
        out_ref, total = refs[-2:]
        k = pl.program_id(0)
        if cols % 128 == 0:
            left = jnp.concatenate([r[0] for r in lefts], axis=1)
            right = jnp.concatenate([r[0] for r in rights], axis=1)
            step = dot(left, right, ((1,), (1,)))
        else:
            step = sum(dot(a[0, 0], b[0], ((1,), (1,))) for a, b in zip(lefts, rights))

        @pl.when(k == 0)
        def _():
            total[...] = step + refs[2 * len(halves)][...].astype(f32) if extra is not None else step

        @pl.when(k > 0)
        def _():
            total[...] += step

        @pl.when(k == steps - 1)
        def _():
            out_ref[...] = total[...].astype(kind)

    if cols % 128 == 0:
        specs = [pl.BlockSpec((1, n, cols), lambda k, s: (s[count], 0, k)) for _ in halves]
    else:
        halves = [h.reshape(h.shape[0], n, steps, cols).transpose(0, 2, 1, 3) for h in halves]
        specs = [pl.BlockSpec((1, 1, n, cols), lambda k, s: (s[count], k, 0, 0)) for _ in halves]
    for h in range(len(halves)):
        specs.append(pl.BlockSpec((1, wide, cols), lambda k, s, h=h: (s[h * steps + k], 0, 0)))
    args = [*halves, *[blocks] * len(halves)]
    if extra is not None:
        specs.append(pl.BlockSpec((n, wide), lambda k, s: (0, 0)))
        args.append(extra)
    return pl.pallas_call(
        body,
        out_shape=jax.ShapeDtypeStruct((n, wide), kind),
        grid_spec=pltpu.PrefetchScalarGridSpec(
            num_scalar_prefetch=1,
            grid=(steps,),
            in_specs=specs,
            out_specs=pl.BlockSpec((n, wide), lambda k, s: (0, 0)),
            scratch_shapes=[pltpu.VMEM((n, wide), f32)],
        ),
        compiler_params=params,
    )(scalars, *args)


def shards(tokens, out_grads, basis_in, basis_out):
    at = {k: lax.axis_index(k) for k in "yzxc"}
    nz, ny = lax.axis_size("z"), lax.axis_size("y")
    width, cols = basis_in.shape
    rows = tokens.shape[0]
    quarter = width // nz
    eighth = quarter // ny

    proj_in = jnp.dot(tokens, basis_in, preferred_element_type=f32).astype(bf16)
    proj_out = jnp.dot(out_grads, basis_out, preferred_element_type=f32).astype(bf16)
    both = jnp.concatenate([proj_in, proj_out], axis=0)
    order = [0] + sorted(range(1, nz), key=lambda s: -min(s, nz - s))
    groups, others, links = {}, {}, []
    for s in order:
        value = fetch(both, "z", s) if s else both
        links += [value] if s else []
        groups[s] = gather(value, "y")
        others[s] = gather(fetch(value[:rows], "x"), "y")
    every = range(nz)
    left, left_other, right = pack([groups[s] for s in every], [others[s] for s in every], rows)
    rights = [right, fetch(right, "c")]

    blocks = pair * pair
    share = quarter // (blocks * ny)
    in_view = basis_in.reshape(nz, blocks, ny, share, cols)
    in_own, in_other = {}, {}
    for s in order:
        to = (at["z"] + nz - s) % nz
        block = lax.dynamic_slice(in_view, (to, 0, at["y"], 0, 0), (1, blocks, 1, share, cols))
        block = block.reshape(eighth, cols)
        in_own[s] = fetch(after(block, *links, in_other[0]), "z", s) if s else block
        in_other[s] = fetch(in_own[s], "x")
    in_own = [in_own[s] for s in range(nz)]
    in_other = [in_other[s] for s in range(nz)]

    out_rows = width // ny
    cuts = [out_rows * sum(shares[:k]) // sum(shares) // 128 * 128 for k in range(len(shares))] + [out_rows]
    sizes = [b - a for a, b in zip(cuts, cuts[1:])]
    wides, gate = [], [*in_own[1:], left]
    for k in range(len(shares)):
        first = at["y"] * out_rows + cuts[k]
        raw = lax.dynamic_slice_in_dim(basis_out, first, sizes[k], 0)
        raw = after(raw, *gate) if gate else raw
        wides.append(lax.all_gather(raw, ("z", "c"), axis=0))

    own = mix(in_own, left, rights, at["c"], 0, 2, f32)
    halves = []
    take = lambda v, axis, i: lax.dynamic_index_in_dim(v, i, axis, keepdims=False)
    for h in range(2):
        part = mix(in_other, left_other, rights, at["c"], h, 1, bf16, own)
        view = part.reshape(pair, pair, share, -1)
        away = fetch(take(view, 1, 1 - at["c"]), "c")
        mine = (take(view, 1, at["c"]).astype(f32) + away.astype(f32)).astype(bf16)
        got = gather(after(mine, *got[1:]) if h else mine, "y")
        full = jnp.stack(
            [lax.select_n((ny + j - at["y"]) % ny, *got) if ny > 2 else
             jnp.where(at["y"] == j, got[0], got[-1]) for j in range(ny)], axis=1)
        halves.append(full.reshape(pair, ny * share, -1))
    place = [
        ((at["z"] + h * (nz // 2) + s) % nz) * pair + j
        for h in range(2) for j in range(pair) for s in range(nz // 2)
    ]
    place = jnp.stack(place).astype(jnp.int32)

    done = []
    for k in range(len(shares)):
        wide = after(wides[k], kept) if k else wides[k]
        given = fetch(expand(halves, 1 - at["x"], wide, place, bf16), "x")
        kept = expand(halves, at["x"], wide, place, f32)
        done.append((kept + given.astype(f32)).astype(bf16))
    return jnp.concatenate(done, axis=1)


def solution(mesh):
    sizes = (mesh.shape["dp"], mesh.shape["panel"] // (pair * pair), pair, pair)
    grid = jax.sharding.Mesh(mesh.devices.reshape(sizes), ("y", "z", "x", "c"))
    panels = ("z", "x", "c")
    return jax.shard_map(
        shards,
        mesh=grid,
        in_specs=(P("y", None), P("y", None), P(None, panels), P(None, panels)),
        out_specs=P(panels, "y"),
        check_vma=False,
    )
```

```python
import jax
import jax.numpy as jnp
from jax import lax
from jax.experimental import pallas as pl
from jax.experimental.pallas import tpu as pltpu
from jax.sharding import PartitionSpec as P

damping = 0.1
pair = 2
shares = (3, 1)
f32 = jnp.float32
bf16 = jnp.bfloat16
params = pltpu.CompilerParams(vmem_limit_bytes=48 * 2**20)


def pairs(size, shift):
    return [((i + shift) % size, i) for i in range(size)]


def fetch(value, axis, shift=1):
    return lax.ppermute(value, axis, pairs(lax.axis_size(axis), shift))


def gather(value, axis):
    return [value] + [fetch(value, axis, s) for s in range(1, lax.axis_size(axis))]


def dot(a, b, contract):
    return lax.dot_general(a, b, (contract, ((), ())), preferred_element_type=f32)


def after(value, *others):
    return pl.pallas_call(
        lambda *refs: None,
        out_shape=jax.ShapeDtypeStruct(value.shape, value.dtype),
        in_specs=[pl.BlockSpec(memory_space=pl.ANY)] * (1 + len(others)),
        out_specs=pl.BlockSpec(memory_space=pl.ANY),
        input_output_aliases={0: 0},
    )(value, *others)


def square(v):
    return (v.astype(f32) ** 2).astype(bf16)


def pack(groups, others, rows):
    count, wide = len(groups), len(groups[0])
    cols = groups[0][0].shape[1]

    def body(*refs):
        left_ref, other_ref, right_ref = refs[-3:]
        for s in range(count):
            for g in range(wide):
                ref = refs[s * wide + g]
                span = slice(g * rows, (g + 1) * rows)
                left_ref[s, :, span] = ref[:rows, :].T
                right_ref[span, s * cols : (s + 1) * cols] = ref[rows:, :]
                other_ref[s, :, span] = refs[(count + s) * wide + g][...].T

    left = jax.ShapeDtypeStruct((count, cols, wide * rows), bf16)
    return pl.pallas_call(
        body,
        out_shape=[left, left, jax.ShapeDtypeStruct((wide * rows, count * cols), bf16)],
        compiler_params=params,
    )(*[v for group in groups + others for v in group])


def mix(rows, left, rights, first, start, runs, kind, carry=None):
    count, cols, tok = left.shape
    n = rows[0].shape[0]
    tj = rights[0].shape[1] // 2
    group = 2 if count % 2 == 0 and cols % 128 == 0 else 1

    def body(first_ref, *refs):
        row_refs, left_ref, refs = refs[:count], refs[count], refs[count + 1 :]
        right_refs, out_ref = refs[: len(rights)], refs[-1]
        j = pl.program_id(0)
        b = jnp.where(j % 2 == first_ref[0], right_refs[0][...], right_refs[1][...])
        b2 = square(b)
        total = refs[len(rights)][...] if carry is not None else None
        for k in range(0, count, group):
            a = left_ref[k : k + group].reshape(group * cols, tok)
            summed = jnp.dot(a, b, preferred_element_type=f32)
            moment = jnp.dot(square(a), b2, preferred_element_type=f32)
            ratio = (summed / (moment + damping * tok)).astype(bf16)
            lead = [row_refs[k + i][...] for i in range(group)]
            lead = jnp.concatenate(lead, axis=1) if group > 1 else lead[0]
            step = jnp.dot(lead, ratio, preferred_element_type=f32)
            total = step if total is None else total + step
        out_ref[...] = total.astype(kind)

    specs = [pl.BlockSpec((n, cols), lambda j, f: (0, 0)) for _ in rows]
    specs += [pl.BlockSpec((count, cols, tok), lambda j, f: (0, 0, 0))]
    specs += [pl.BlockSpec((tok, tj), lambda j, f: (0, start + j // 2)) for _ in rights]
    args = [*rows, left, *rights]
    if carry is not None:
        specs.append(pl.BlockSpec((n, tj), lambda j, f: (0, 2 * start + j)))
        args.append(carry)
    return pl.pallas_call(
        body,
        out_shape=jax.ShapeDtypeStruct((n, 2 * runs * tj), kind),
        grid_spec=pltpu.PrefetchScalarGridSpec(
            num_scalar_prefetch=1,
            grid=(2 * runs,),
            in_specs=specs,
            out_specs=pl.BlockSpec((n, tj), lambda j, f: (0, j)),
        ),
        compiler_params=params,
    )(jnp.full((1,), first, jnp.int32), *args)


def expand(halves, pick, blocks, order, kind, extra=None):
    _, n, deep = halves[0].shape
    count, wide, cols = blocks.shape
    steps = count // len(halves)
    scalars = jnp.concatenate([order, jnp.full((1,), pick, jnp.int32)])

    def body(scalar_ref, *refs):
        lefts, rights = refs[: len(halves)], refs[len(halves) : 2 * len(halves)]
        out_ref, total = refs[-2:]
        k = pl.program_id(0)
        if cols % 128 == 0:
            left = jnp.concatenate([r[0] for r in lefts], axis=1)
            right = jnp.concatenate([r[0] for r in rights], axis=1)
            step = dot(left, right, ((1,), (1,)))
        else:
            step = sum(dot(a[0, 0], b[0], ((1,), (1,))) for a, b in zip(lefts, rights))

        @pl.when(k == 0)
        def _():
            total[...] = step + refs[2 * len(halves)][...].astype(f32) if extra is not None else step

        @pl.when(k > 0)
        def _():
            total[...] += step

        @pl.when(k == steps - 1)
        def _():
            out_ref[...] = total[...].astype(kind)

    if cols % 128 == 0:
        specs = [pl.BlockSpec((1, n, cols), lambda k, s: (s[count], 0, k)) for _ in halves]
    else:
        halves = [h.reshape(h.shape[0], n, steps, cols).transpose(0, 2, 1, 3) for h in halves]
        specs = [pl.BlockSpec((1, 1, n, cols), lambda k, s: (s[count], k, 0, 0)) for _ in halves]
    for h in range(len(halves)):
        specs.append(pl.BlockSpec((1, wide, cols), lambda k, s, h=h: (s[h * steps + k], 0, 0)))
    args = [*halves, *[blocks] * len(halves)]
    if extra is not None:
        specs.append(pl.BlockSpec((n, wide), lambda k, s: (0, 0)))
        args.append(extra)
    return pl.pallas_call(
        body,
        out_shape=jax.ShapeDtypeStruct((n, wide), kind),
        grid_spec=pltpu.PrefetchScalarGridSpec(
            num_scalar_prefetch=1,
            grid=(steps,),
            in_specs=specs,
            out_specs=pl.BlockSpec((n, wide), lambda k, s: (0, 0)),
            scratch_shapes=[pltpu.VMEM((n, wide), f32)],
        ),
        compiler_params=params,
    )(scalars, *args)


def shards(tokens, out_grads, basis_in, basis_out):
    at = {k: lax.axis_index(k) for k in "yzxc"}
    nz, ny = lax.axis_size("z"), lax.axis_size("y")
    width, cols = basis_in.shape
    rows = tokens.shape[0]
    quarter = width // nz
    eighth = quarter // ny

    proj_in = jnp.dot(tokens, basis_in, preferred_element_type=f32).astype(bf16)
    proj_out = jnp.dot(out_grads, basis_out, preferred_element_type=f32).astype(bf16)
    both = jnp.concatenate([proj_in, proj_out], axis=0)
    blocks = pair * pair
    share = quarter // (blocks * ny)
    in_view = basis_in.reshape(nz, blocks, ny, share, cols)
    def in_block(s):
        to = (at["z"] + nz - s) % nz
        block = lax.dynamic_slice(in_view, (to, 0, at["y"], 0, 0), (1, blocks, 1, share, cols))
        return block.reshape(eighth, cols)

    early = fetch(in_block(1), "z", 1)
    both = after(both, early)
    order = [0] + sorted(range(1, nz), key=lambda s: -min(s, nz - s))
    groups, others, links = {}, {}, []
    for s in order:
        value = fetch(both, "z", s) if s else both
        links += [value] if s else []
        groups[s] = gather(value, "y")
        others[s] = gather(fetch(value[:rows], "x"), "y")
    every = range(nz)
    left, left_other, right = pack([groups[s] for s in every], [others[s] for s in every], rows)
    rights = [right, fetch(right, "c")]

    in_own, in_other = {}, {}
    for s in order:
        block = in_block(s) if s != 1 else early
        in_own[s] = fetch(after(block, *links, in_other[0]), "z", s) if s > 1 else block
        in_other[s] = fetch(in_own[s], "x")
    in_own = [in_own[s] for s in range(nz)]
    in_other = [in_other[s] for s in range(nz)]

    out_rows = width // ny
    cuts = [out_rows * sum(shares[:k]) // sum(shares) // 128 * 128 for k in range(len(shares))] + [out_rows]
    sizes = [b - a for a, b in zip(cuts, cuts[1:])]
    wides, gate = [], [*in_own[1:], *[w for s in order[:-1] for w in others[s][1:]], others[order[-1]][0], *[w for s in order for w in groups[s][1:]]]
    for k in range(len(shares)):
        first = at["y"] * out_rows + cuts[k]
        raw = lax.dynamic_slice_in_dim(basis_out, first, sizes[k], 0)
        raw = after(raw, *gate) if gate else raw
        wides.append(lax.all_gather(raw, ("z", "c"), axis=0))

    own = mix(in_own, left, rights, at["c"], 0, 2, f32)
    halves = []
    take = lambda v, axis, i: lax.dynamic_index_in_dim(v, i, axis, keepdims=False)
    for h in range(2):
        part = mix(in_other, left_other, rights, at["c"], h, 1, bf16, own)
        view = part.reshape(pair, pair, share, -1)
        away = take(view, 1, 1 - at["c"])
        away = jnp.stack([fetch(away[i], "c") for i in range(pair)])
        mine = (take(view, 1, at["c"]).astype(f32) + away.astype(f32)).astype(bf16)
        got = gather(after(mine, *got[1:]) if h else mine, "y")
        full = jnp.stack(
            [lax.select_n((ny + j - at["y"]) % ny, *got) if ny > 2 else
             jnp.where(at["y"] == j, got[0], got[-1]) for j in range(ny)], axis=1)
        halves.append(full.reshape(pair, ny * share, -1))
    place = [
        ((at["z"] + h * (nz // 2) + s) % nz) * pair + j
        for h in range(2) for j in range(pair) for s in range(nz // 2)
    ]
    place = jnp.stack(place).astype(jnp.int32)

    done = []
    for k in range(len(shares)):
        wide = after(wides[k], kept) if k else wides[k]
        given = fetch(expand(halves, 1 - at["x"], wide, place, bf16), "x")
        kept = expand(halves, at["x"], wide, place, f32)
        done.append((kept + given.astype(f32)).astype(bf16))
    return jnp.concatenate(done, axis=1)


def solution(mesh):
    sizes = (mesh.shape["dp"], mesh.shape["panel"] // (pair * pair), pair, pair)
    grid = jax.sharding.Mesh(mesh.devices.reshape(sizes), ("y", "z", "x", "c"))
    panels = ("z", "x", "c")
    return jax.shard_map(
        shards,
        mesh=grid,
        in_specs=(P("y", None), P("y", None), P(None, panels), P(None, panels)),
        out_specs=P(panels, "y"),
        check_vma=False,
    )
```
